128 devices in a mesh: row: 16 (over y, z), col: 8 (over x, core).
Axes of the slice: x: 4, y: 4, z: 4, core: 2. Of those that a mesh axis runs over, the one named last changes fastest.
Arguments:
- trailing_block: float32 [2, 16, 512, 4, 8, 512], P(None, 'row', None, None, 'col'), may hold values from -6 to 6
- panel_block: float32 [2, 16, 512, 1024], P(None, 'row', None, 'col'), may hold values from -0.9 to 0.9
- inv_factor: float32 [1024, 1024], replicated, as said below
Outputs:
- updated: float32 [2, 16, 512, 4, 8, 512], P(None, 'row', None, None, 'col')
- factor_panel: float32 [2, 16, 512, 1024], P(None, 'row', None, 'col')
The draws below stay inside these ranges and needn't reach their ends.
Inputs may be any that keep to these rules, and one draw needn't show every extreme that they name: `inv_factor`: lower triangular; diagonal entries lie between 1 and 2.
All inputs are finite; a program needn't handle non-finite values.
Results may differ from the reference program's by a relative error of at most 0.00007.
Values sent between devices are 32-bit elements; how exact they have to be, the bound alone decides.
No kernel may reach another device: no remote copies, remote signals or barrier semaphores. Data moves between devices by JAX's collectives and lax.ppermute only.
A program may use at most 128 MiB of HBM per device.

```python
import math
import jax
import jax.numpy as jnp
from jax import lax

NB = 512
P_SIZE = 1024
ORDER = 16384
RT = 2
CT = 4
N_ROW = 16
N_COL = 8


def draw_inv_factor(key, part):
    key = jax.random.fold_in(key, 7)
    key_off, key_diag = jax.random.split(key)
    rows_idx = lax.broadcasted_iota(jnp.int32, (P_SIZE, P_SIZE), 0)
    cols_idx = lax.broadcasted_iota(jnp.int32, (P_SIZE, P_SIZE), 1)
    off_part = jax.random.normal(key_off, (P_SIZE, P_SIZE), jnp.float32)
    diag_part = jax.random.uniform(key_diag, (P_SIZE, P_SIZE), jnp.float32, 1.0, 2.0)
    lower = jnp.where(rows_idx > cols_idx, off_part / math.sqrt(P_SIZE), 0.0)
    result = jnp.where(rows_idx == cols_idx, diag_part, lower)
    return result.astype(jnp.float32)


def shard_levels(key, extent, pieces, low, high):
    level, own = 1.0, jax.random.fold_in(key, 6)
    for axis_at, blocks in pieces:
        heights = jnp.exp(jax.random.uniform(jax.random.fold_in(own, axis_at), (blocks,), jnp.float32, low / len(pieces), high / len(pieces)))
        level = level * jnp.repeat(heights, extent[axis_at] // blocks).reshape([-1 if axis == axis_at else 1 for axis in range(len(extent))])
    return level


def normal_values(rng, dims, scale, bound, pieces=(), dtype=jnp.bfloat16):
    drawn = scale * jax.random.normal(rng, dims, jnp.float32)
    if pieces:
        drawn = drawn * shard_levels(rng, dims, pieces, -0.22, 0.18)
    return jnp.clip(drawn, -bound, bound).astype(dtype)


def setup_inputs(seed: int = 0) -> dict:
    key_of = jax.random.split(jax.random.key(seed), 4)
    return {
        "trailing_block": normal_values(key_of[0], (RT, N_ROW, NB, CT, N_COL, NB), 1.0, 6.0, ((1, 16), (4, 8)), jnp.float32),
        "panel_block": normal_values(key_of[1], (RT, N_ROW, NB, P_SIZE), 0.15, 0.9, ((1, 16), (3, 8)), jnp.float32),
        "inv_factor": draw_inv_factor(jax.random.fold_in(key_of[3], 71), 0),
    }


def reference(trailing_block, panel_block, inv_factor):
    matrix = trailing_block.reshape(ORDER, ORDER)
    panel_rows = panel_block.reshape(ORDER, P_SIZE)
    factor = jnp.dot(panel_rows, inv_factor.T, precision=lax.Precision.HIGHEST, preferred_element_type=jnp.float32)
    updated = matrix - jnp.dot(factor, factor.T, precision=lax.Precision.HIGHEST, preferred_element_type=jnp.float32)
    return updated.reshape(trailing_block.shape), factor.reshape(panel_block.shape)
```

```python
import functools

import jax
import jax.numpy as jnp
from jax import lax
from jax.experimental import pallas as pl
from jax.experimental.pallas import tpu as pltpu
from jax.sharding import PartitionSpec as P

BOTH = ("row", "col")
F32, BF16 = jnp.float32, jnp.bfloat16
LAST = (((1,), (1,)), ((), ()))
PLAIN = (((1,), (0,)), ((), ()))
VMEM_LIMIT = 56 * 1024 * 1024


def device_index(x, y, z, core):
    return (y * 4 + z) * 8 + x * 2 + core


def permutation(move):
    pairs = []
    for x in range(4):
        for y in range(4):
            for z in range(4):
                for core in range(2):
                    to_y, to_z = move(y, z, core)
                    pairs.append(
                        (device_index(x, y, z, core), device_index(x, to_y % 4, to_z % 4, core))
                    )
    return pairs


def first_axis(step):
    return permutation(lambda y, z, core: (y, z + step) if core == 0 else (y + step, z))


def second_axis(step):
    return permutation(lambda y, z, core: (y + step, z) if core == 0 else (y, z + step))


def spread():
    pairs = []
    for half in range(2):
        for k in range(8):
            for c in range(8):
                pairs.append(((8 * half + c) * 8 + k, (8 * half + k) * 8 + c))
    return pairs


def ring(block, axis):
    rows = block.shape[0] // 2
    ahead = lax.ppermute(block, BOTH, axis(-1))
    behind = lax.ppermute(block, BOTH, axis(1))
    far_top = lax.ppermute(ahead[:rows], BOTH, axis(-1))
    far_bottom = lax.ppermute(behind[rows:], BOTH, axis(1))
    return ahead, behind, far_top, far_bottom


def split(value):
    high = value.astype(BF16)
    return high, (value - high.astype(F32)).astype(BF16)


def dot3(left, right, dims):
    dot = functools.partial(lax.dot_general, dimension_numbers=dims, preferred_element_type=F32)
    return dot(left[0], right[0]) + (dot(left[0], right[1]) + dot(left[1], right[0]))


def factor_kernel(col_ref, rows_ref, inv_ref, own_ref, ghi_ref, glo_ref, f_ref, bhi, blo, lhi, llo):
    wide = 256
    count = inv_ref.shape[0] // wide
    for k in range(2 * count):
        high, low = split(rows_ref[k])
        bhi[:, k * 128 : (k + 1) * 128] = high
        blo[:, k * 128 : (k + 1) * 128] = low
    high, low = split(inv_ref[...])
    lhi[...] = high
    llo[...] = low

    def cut(at):
        return slice(at * wide, (at + 1) * wide)

    for j in range(count):
        upto = slice(0, (j + 1) * wide)
        f_ref[:, cut(j)] = dot3(
            (bhi[:, upto], blo[:, upto]), (lhi[cut(j), upto], llo[cut(j), upto]), LAST
        )
    start = pl.multiple_of(col_ref[0] * 128, 128)
    own_ref[...] = f_ref[:, pl.ds(start, 128)]
    high, low = split(f_ref[...])
    bhi[...] = high
    blo[...] = low
    for k in range(count):
        onward = slice(k * wide, count * wide)
        total = dot3(
            (bhi[:, onward], blo[:, onward]), (lhi[onward, cut(k)], llo[onward, cut(k)]), PLAIN
        )
        high, low = split(total)
        ghi_ref[:, cut(k)] = high
        glo_ref[:, cut(k)] = low


def factor(col_index, rows, inv_factor):
    count, local, _ = rows.shape
    order = inv_factor.shape[0]
    vmem = pl.BlockSpec(memory_space=pltpu.VMEM)
    return pl.pallas_call(
        factor_kernel,
        out_shape=(
            jax.ShapeDtypeStruct((local, 128), F32),
            jax.ShapeDtypeStruct((local, order), BF16),
            jax.ShapeDtypeStruct((local, order), BF16),
        ),
        in_specs=[pl.BlockSpec(memory_space=pltpu.SMEM), vmem, vmem],
        out_specs=(vmem, vmem, vmem),
        scratch_shapes=[
            pltpu.VMEM((local, order), F32),
            pltpu.VMEM((local, order), BF16),
            pltpu.VMEM((local, order), BF16),
            pltpu.VMEM((order, order), BF16),
            pltpu.VMEM((order, order), BF16),
        ],
        compiler_params=pltpu.CompilerParams(vmem_limit_bytes=VMEM_LIMIT),
        cost_estimate=pl.CostEstimate(
            flops=2 * 3 * local * order * order, bytes_accessed=13 * 2**20, transcendentals=0
        ),
    )(col_index, rows, inv_factor)


def update_kernel(place_ref, ghi, glo, held, ahead, behind, top, bottom, a_ref, *rest):
    out_ref, b_ref, bhi, blo, sems = rest[-5:]
    block_rows = a_ref.shape[0]
    tile = 512

    @pl.when(pl.program_id(0) == 0)
    def _():
        copies = []
        for ref in (held, ahead, behind, top, bottom):
            for part in range(ref.shape[0] // tile):
                at = len(copies)
                place = place_ref[at]
                row = pl.multiple_of((place // 8) * tile, tile)
                lane = pl.multiple_of((place % 8) * 128, 128)
                copy = pltpu.make_async_copy(
                    ref.at[pl.ds(part * tile, tile), :],
                    b_ref.at[pl.ds(row, tile), pl.ds(lane, 128)],
                    sems.at[at],
                )
                copy.start()
                copies.append(copy)
        for copy in copies:
            copy.wait()
        high, low = split(b_ref[...])
        bhi[...] = high
        blo[...] = low

    a_rows = a_ref.reshape(block_rows * 8, 128)
    out_rows = out_ref.reshape(block_rows * 8, 128)
    for n in range(4):
        cols = slice(n * 256, (n + 1) * 256)
        product = dot3((ghi[...], glo[...]), (bhi[cols, :], blo[cols, :]), LAST)
        for j in range(2):
            lines = pl.ds(2 * n + j, block_rows, 8)
            out_rows[lines, :] = a_rows[lines, :] - product[:, j * 128 : (j + 1) * 128]


def update(part, place, g, received, trailing, so_far):
    local, order = g[0].shape
    block_rows = 256
    g_spec = pl.BlockSpec((block_rows, order), lambda i, place: (i, 0))
    a_spec = pl.BlockSpec((block_rows, 8, 128), lambda i, place: (i, part, 0))
    hbm = pl.BlockSpec(memory_space=pl.ANY)
    operands = [place, *g, *received, trailing]
    in_specs = [g_spec, g_spec, *[hbm] * len(received), a_spec]
    aliases = {}
    if so_far is not None:
        aliases = {len(operands): 0}
        operands.append(so_far)
        in_specs.append(hbm)
    return pl.pallas_call(
        update_kernel,
        out_shape=jax.ShapeDtypeStruct(trailing.shape, F32),
        grid_spec=pltpu.PrefetchScalarGridSpec(
            num_scalar_prefetch=1,
            grid=(local // block_rows,),
            in_specs=in_specs,
            out_specs=a_spec,
            scratch_shapes=[
                pltpu.VMEM((1024, order), F32),
                pltpu.VMEM((1024, order), BF16),
                pltpu.VMEM((1024, order), BF16),
                pltpu.SemaphoreType.DMA((16,)),
            ],
        ),
        input_output_aliases=aliases,
        compiler_params=pltpu.CompilerParams(vmem_limit_bytes=VMEM_LIMIT),
        cost_estimate=pl.CostEstimate(
            flops=2 * 3 * local * 1024 * order, bytes_accessed=16 * 2**20, transcendentals=0
        ),
    )(*operands)


def places():
    row, core = lax.axis_index("row"), lax.axis_index("col") % 2
    y, z = row // 4, row % 4
    order = [(0, s) for s in range(4)] + [(1, s) for s in range(4)]
    order += [(3, s) for s in range(4)] + [(2, s) for s in range(4)]
    steps = (0, 1, 3, 2)
    second = jnp.array([d for d, _ in order], jnp.int32)
    first = jnp.array([steps[s] for _, s in order], jnp.int32)
    at_y = (y + jnp.where(core == 0, second, first)) % 4
    at_z = (z + jnp.where(core == 0, first, second)) % 4
    return at_y * 4 + at_z


def per_device(trailing_block, panel_block, inv_factor):
    tiles, _, tile, cols_dev = panel_block.shape
    local = tiles * tile
    panel = panel_block.reshape(tiles, tile, cols_dev)
    trailing = trailing_block.reshape(local, 16, 128)
    col_index = lax.axis_index("col").astype(jnp.int32).reshape(1)
    rows = lax.all_gather(panel.reshape(local, cols_dev), "col", axis=0)
    place = places()
    received = []
    for part in range(tiles):
        own = lax.ppermute(panel[part], BOTH, spread())
        held = jnp.concatenate([own, *ring(own, first_axis)], axis=0)
        received.append((held, *ring(held, second_axis)))
    own_columns, *g = factor(col_index, rows, inv_factor)
    updated = None
    for part in range(tiles):
        updated = update(part, place, g, received[part], trailing, updated)
    return updated.reshape(trailing_block.shape), own_columns.reshape(panel_block.shape)


def solution(mesh):
    return jax.shard_map(
        per_device,
        mesh=mesh,
        in_specs=(P(None, "row", None, None, "col", None), P(None, "row", None, "col"), P()),
        out_specs=(P(None, "row", None, None, "col", None), P(None, "row", None, "col")),
        check_vma=False,
    )
```

```python
import functools

import jax
import jax.numpy as jnp
from jax import lax
from jax.experimental import pallas as pl
from jax.experimental.pallas import tpu as pltpu
from jax.sharding import PartitionSpec as P

BOTH = ("row", "col")
F32, BF16 = jnp.float32, jnp.bfloat16
LAST = (((1,), (1,)), ((), ()))
GF_FACTOR, GF_UPDATE = 4.0, 2.0
LIM = 44


def permutation(move):
    def index(x, y, z, core):
        return (y % 4 * 4 + z % 4) * 8 + x % 4 * 2 + core

    spots = [(x, y, z, core) for x in range(4) for y in range(4) for z in range(4) for core in (0, 1)]
    return [(index(*spot), index(*move(*spot))) for spot in spots]


def first_axis(step):
    return permutation(lambda x, y, z, core: (x, y + core * step, z + (1 - core) * step, core))


def second_axis(step):
    return permutation(lambda x, y, z, core: (x, y + (1 - core) * step, z + core * step, core))


def x_axis(step):
    return permutation(lambda x, y, z, core: (x + step, y, z, core))


OUTWARD = permutation(lambda x, y, z, core: (x - 1 + 2 * core, y, z, core))
SWAP = permutation(lambda x, y, z, core: (x, y, z, 1 - core))


def split(value):
    high = value.astype(BF16)
    return high, (value - high.astype(F32)).astype(BF16)


def dot3(left, right):
    dot = functools.partial(lax.dot_general, dimension_numbers=LAST, preferred_element_type=F32)
    return dot(left[0], right[0]) + (dot(left[0], right[1]) + dot(left[1], right[0]))


def call(kernel, out_shape, operands, in_specs, out_specs, scratch, megabytes, gigaflops, aliases=None):
    return pl.pallas_call(
        kernel,
        out_shape=out_shape,
        in_specs=in_specs,
        out_specs=out_specs,
        scratch_shapes=scratch,
        input_output_aliases=aliases or {},
        compiler_params=pltpu.CompilerParams(vmem_limit_bytes=megabytes * 2**20),
        cost_estimate=pl.CostEstimate(
            flops=int(gigaflops * 1e9), bytes_accessed=2**20, transcendentals=0
        ),
    )(*operands)


VMEM = pl.BlockSpec(memory_space=pltpu.VMEM)
ANY = pl.BlockSpec(memory_space=pl.ANY)


def place():
    row, col = lax.axis_index("row"), lax.axis_index("col")
    return col >> 1, col & 1, row >> 2, row & 3


def fetch_inverse(inv_hbm, inv_ref, sems, pieces):
    copies, wide = [], 256
    for j in range(inv_ref.shape[0] // wide):
        copies.append([])
        for at in range(pieces):
            tall = wide // pieces
            spot = (pl.ds(j * wide + at * tall, tall), pl.ds(0, (j + 1) * wide))
            copies[j].append(
                pltpu.make_async_copy(inv_hbm.at[spot], inv_ref.at[spot], sems.at[j, at])
            )
            copies[j][-1].start()
    return copies


def turn_kernel(rows_ref, out_ref):
    _, _, _, z = place()
    for at in range(8):
        turned = (at % 2) * 4 + at // 2 % 2 * 2 + at // 4
        out_ref[at] = rows_ref[jnp.where((z & 1) == 1, turned, at)]


def turn(rows):
    out = jax.ShapeDtypeStruct(rows.shape, F32)
    return call(turn_kernel, out, (rows,), [VMEM], VMEM, [], LIM, 0.5)


def slice_kernel(rows_ref, inv_ref, out_ref, bhi, blo):
    for k in range(rows_ref.shape[0]):
        high, low = split(rows_ref[k])
        bhi[:, k * 128 : (k + 1) * 128] = high
        blo[:, k * 128 : (k + 1) * 128] = low
    for j in range(inv_ref.shape[0] // 256):
        cols, upto = slice(j * 256, (j + 1) * 256), slice(0, (j + 1) * 256)
        out_ref[:, cols] = dot3((bhi[:, upto], blo[:, upto]), split(inv_ref[cols, upto]))


def factor_slice(rows, inv_factor):
    count, tall, _ = rows.shape
    order = inv_factor.shape[0]
    return call(
        slice_kernel,
        jax.ShapeDtypeStruct((tall, order), F32),
        (rows, inv_factor),
        [VMEM, VMEM],
        VMEM,
        [pltpu.VMEM((tall, order), BF16), pltpu.VMEM((tall, order), BF16)],
        LIM,
        0.5,
    )


def factor_kernel(*rest):
    x, core, _, _ = place()
    order = [(0, 0), (0, 1)] + [(step, side) for side in (0, 1) for step in (1, 3, 2)]
    pieces, rest = rest[:-11], rest[-11:]
    inv_hbm, own_ref, halves, line_ref, f_ref, bhi, blo, inv_ref, lhi, llo, sems = rest
    local, step = line_ref.shape[1], 256
    copies = []
    for ref in pieces:
        for piece in range(ref.shape[0] // local):
            at = len(copies)
            rows = pl.ds(piece * local, local)
            copies.append(pltpu.make_async_copy(ref.at[rows, :], line_ref.at[at], sems.at[0, at // 2, at % 2]))
            copies[-1].start()
    ready = fetch_inverse(inv_hbm, inv_ref, sems.at[1], 2)
    for at, copy in enumerate(copies):
        copy.wait()
        step_x, side = order[at]
        lane = pl.multiple_of((((x + step_x) & 3) * 2 + (core ^ side)) * 128, 128)
        high, low = split(line_ref[at])
        bhi[:, pl.ds(lane, 128)] = high
        blo[:, pl.ds(lane, 128)] = low
    for m in range(local // step):
        rows = slice(m * step, (m + 1) * step)
        for j, arriving in enumerate(ready):
            cols, upto = slice(j * 256, (j + 1) * 256), slice(0, (j + 1) * 256)
            if m == 0:
                for copy in arriving:
                    copy.wait()
                high, low = split(inv_ref[cols, upto])
                lhi[cols, upto] = high
                llo[cols, upto] = low
            value = dot3((bhi[rows, upto], blo[rows, upto]), (lhi[cols, upto], llo[cols, upto]))
            high, low = split(value)
            halves[0, rows, cols] = high
            halves[1, rows, cols] = low
            for side in range(2):
                f_ref[2 * j + side, rows, :] = value[:, side * 128 : (side + 1) * 128]
    own_ref[...] = f_ref[x * 2 + core]


def factor(pieces, inv_factor):
    local, order = pieces[0].shape[0], inv_factor.shape[0]
    return call(
        factor_kernel,
        (
            jax.ShapeDtypeStruct((local, 128), F32),
            jax.ShapeDtypeStruct((2, local, order), BF16),
        ),
        (*pieces, inv_factor),
        [ANY] * (len(pieces) + 1),
        (VMEM, VMEM),
        [
            pltpu.VMEM((order // 128, local, 128), F32),
            pltpu.VMEM((order // 128, local, 128), F32),
            pltpu.VMEM((local, order), BF16),
            pltpu.VMEM((local, order), BF16),
            pltpu.VMEM((order, order), F32),
            pltpu.VMEM((order, order), BF16),
            pltpu.VMEM((order, order), BF16),
            pltpu.SemaphoreType.DMA((2, 4, 2)),
        ],
        LIM,
        GF_FACTOR,
    )


NEAR, FAR = (0, 1), (3, 2)


def update_kernel(sources, f_ref, *rest):
    pieces, (a_ref, out_ref, buf, chi, clo, sems) = rest[:2], (rest[2], *rest[-5:])
    _, core, y, z = place()
    first, second = jnp.where(core == 0, z, y), jnp.where(core == 0, y, z)
    spot = []
    for move, steps in sources:
        p = (second + move) & 3
        for step in steps:
            q = (first + step) & 3
            other = (q >> 1) * 4 + (p >> 1) * 2 + (q & 1)
            spot.append(jnp.where(core == 0, (p >> 1) * 4 + q, other))
    local, step = buf.shape[0], 256
    group = pl.multiple_of(((second + sources[0][0]) & 1) * 8, 8)
    ins, outs = [], []
    for m in range(local // step):
        lines = pl.ds(m * step, step)
        here = a_ref.at[lines, pl.ds(group, 8), :]
        there = out_ref.at[lines, pl.ds(group, 8), :]
        ins.append(pltpu.make_async_copy(here, buf.at[lines], sems.at[0, m]))
        outs.append(pltpu.make_async_copy(buf.at[lines], there, sems.at[1, m]))
    for copy in ins:
        copy.start()
    for at, ref in enumerate(pieces):
        rows = slice(at * 256, (at + 1) * 256)
        high, low = split(ref[...])
        chi[rows, :] = high
        clo[rows, :] = low
    flat = buf.reshape(local * 8, 128)
    for m in range(local // step):
        lines = pl.ds(m * step, step)
        ins[m].wait()
        for n in range(2):
            cols = slice(n * 256, (n + 1) * 256)
            product = dot3((f_ref[0, lines, :], f_ref[1, lines, :]), (chi[cols, :], clo[cols, :]))
            for j in range(2):
                spots = pl.ds(m * step * 8 + spot[2 * n + j], step, 8)
                flat[spots, :] = flat[spots, :] - product[:, j * 128 : (j + 1) * 128]
        outs[m].start()
    for copy in outs:
        copy.wait()


def update(sources, f, pieces, source, so_far):
    _, local, order = f.shape
    operands = [f, *pieces, source]
    in_specs = [VMEM, VMEM, VMEM, ANY]
    aliases = {3: 0}
    if so_far is not source:
        aliases = {}
        if so_far is not None:
            aliases = {4: 0}
            operands.append(so_far)
            in_specs.append(ANY)
    return call(
        functools.partial(update_kernel, sources),
        jax.ShapeDtypeStruct(source.shape, F32),
        operands,
        in_specs,
        ANY,
        [
            pltpu.VMEM((local, 8, 128), F32),
            pltpu.VMEM((512, order), BF16),
            pltpu.VMEM((512, order), BF16),
            pltpu.SemaphoreType.DMA((2, local // 256)),
        ],
        LIM,
        GF_UPDATE,
        aliases,
    )


def pick_kernel(even_ref, odd_ref, out_ref):
    _, core, _, _ = place()

    @pl.when(core == 0)
    def _():
        out_ref[...] = even_ref[...]

    @pl.when(core == 1)
    def _():
        out_ref[...] = odd_ref[...]


def pick(even, odd):
    out = jax.ShapeDtypeStruct(even.shape, F32)
    return call(pick_kernel, out, (even, odd), [VMEM, VMEM], VMEM, [], LIM, 0.1)


def join_kernel(*refs):
    *parts, out_ref = refs
    rows = parts[0].shape[0]
    for at, part in enumerate(parts):
        out_ref[at * rows : (at + 1) * rows] = part[...]


def join(*parts):
    rows, cols = parts[0].shape
    return call(
        join_kernel,
        jax.ShapeDtypeStruct((len(parts) * rows, cols), F32),
        parts,
        [VMEM] * len(parts),
        VMEM,
        [],
        LIM,
        0.1,
    )


def per_device(trailing_block, panel_block, inv_factor):
    tiles, _, tile, cols_dev = panel_block.shape
    local = tiles * tile
    panel = panel_block.reshape(local, cols_dev)
    trailing = trailing_block.reshape(local, 16, 128)

    swapped = lax.ppermute(panel, BOTH, SWAP)
    line_ahead = lax.ppermute(panel, BOTH, x_axis(-1))
    line_behind = lax.ppermute(panel, BOTH, x_axis(1))
    mine = turn(panel.reshape(8, 128, cols_dev))
    halves = [list(range(8)), list(range(8, 16))]
    mine = lax.all_to_all(mine, "row", 0, 0, axis_index_groups=halves, tiled=True)
    mine, line_ahead, line_behind = lax.optimization_barrier((mine, line_ahead, line_behind))
    line_across = lax.ppermute(pick(line_ahead, line_behind), BOTH, OUTWARD)
    mine = lax.all_to_all(mine, "col", 0, 0, tiled=True)
    own = factor_slice(mine, inv_factor)

    ahead = lax.ppermute(own, BOTH, first_axis(-1))
    behind = lax.ppermute(own, BOTH, first_axis(1))
    across = lax.ppermute(own, BOTH, first_axis(2))

    line_ahead, line_behind, line_across, _ = lax.optimization_barrier(
        (line_ahead, line_behind, line_across, own)
    )
    others = join(line_ahead, line_behind, line_across)
    line = (panel, swapped, others, lax.ppermute(others, BOTH, SWAP))
    own_columns, f = factor(line, inv_factor)

    ahead, behind, across, f = lax.optimization_barrier((ahead, behind, across, f))
    near = join(own, ahead)
    near_ahead = lax.ppermute(near, BOTH, second_axis(-1))
    near_behind = lax.ppermute(near, BOTH, second_axis(1))
    far = join(behind, across)
    far_behind = lax.ppermute(far, BOTH, second_axis(1))
    far_ahead = lax.ppermute(far, BOTH, second_axis(-1))
    updated = update(((0, NEAR), (0, FAR)), f, (near, far), trailing, None)
    near_ahead, far_behind, updated = lax.optimization_barrier((near_ahead, far_behind, updated))
    near_across = lax.ppermute(near_ahead, BOTH, second_axis(-1))
    far_across = lax.ppermute(far_behind, BOTH, second_axis(1))

    updated = update(((1, NEAR), (3, FAR)), f, (near_ahead, far_behind), trailing, updated)
    updated = update(((1, FAR), (3, NEAR)), f, (far_ahead, near_behind), updated, updated)
    updated = update(((2, NEAR), (2, FAR)), f, (near_across, far_across), updated, updated)
    return updated.reshape(trailing_block.shape), own_columns.reshape(panel_block.shape)


def solution(mesh):
    return jax.shard_map(
        per_device,
        mesh=mesh,
        in_specs=(P(None, "row", None, None, "col", None), P(None, "row", None, "col"), P()),
        out_specs=(P(None, "row", None, None, "col", None), P(None, "row", None, "col")),
        check_vma=False,
    )
```

```python
import functools

import jax
import jax.numpy as jnp
from jax import lax
from jax.experimental import pallas as pl
from jax.experimental.pallas import tpu as pltpu
from jax.sharding import PartitionSpec as P

BOTH = ("row", "col")
F32, BF16 = jnp.float32, jnp.bfloat16
LAST = (((1,), (1,)), ((), ()))
GF_FACTOR, GF_UPDATE = 4.0, 2.0
LIM = 40


def permutation(move):
    def index(x, y, z, core):
        return (y % 4 * 4 + z % 4) * 8 + x % 4 * 2 + core

    spots = [(x, y, z, core) for x in range(4) for y in range(4) for z in range(4) for core in (0, 1)]
    return [(index(*spot), index(*move(*spot))) for spot in spots]


def first_axis(step):
    return permutation(lambda x, y, z, core: (x, y + core * step, z + (1 - core) * step, core))


def second_axis(step):
    return permutation(lambda x, y, z, core: (x, y + (1 - core) * step, z + core * step, core))


def x_axis(step):
    return permutation(lambda x, y, z, core: (x + step, y, z, core))


OUTWARD = permutation(lambda x, y, z, core: (x - 1 + 2 * core, y, z, core))
SWAP = permutation(lambda x, y, z, core: (x, y, z, 1 - core))


def split(value):
    high = value.astype(BF16)
    return high, (value - high.astype(F32)).astype(BF16)


def dot3(left, right):
    dot = functools.partial(lax.dot_general, dimension_numbers=LAST, preferred_element_type=F32)
    return dot(left[0], right[0]) + (dot(left[0], right[1]) + dot(left[1], right[0]))


def call(kernel, out_shape, operands, in_specs, out_specs, scratch, megabytes, gigaflops, aliases=None):
    return pl.pallas_call(
        kernel,
        out_shape=out_shape,
        in_specs=in_specs,
        out_specs=out_specs,
        scratch_shapes=scratch,
        input_output_aliases=aliases or {},
        compiler_params=pltpu.CompilerParams(vmem_limit_bytes=megabytes * 2**20),
        cost_estimate=pl.CostEstimate(
            flops=int(gigaflops * 1e9), bytes_accessed=2**20, transcendentals=0
        ),
    )(*operands)


VMEM = pl.BlockSpec(memory_space=pltpu.VMEM)
ANY = pl.BlockSpec(memory_space=pl.ANY)


def place():
    row, col = lax.axis_index("row"), lax.axis_index("col")
    return col >> 1, col & 1, row >> 2, row & 3


def fetch_inverse(inv_hbm, inv_ref, sems, pieces):
    copies, wide = [], 256
    for j in range(inv_ref.shape[0] // wide):
        copies.append([])
        for at in range(pieces):
            tall = wide // pieces
            spot = (pl.ds(j * wide + at * tall, tall), pl.ds(0, (j + 1) * wide))
            copies[j].append(
                pltpu.make_async_copy(inv_hbm.at[spot], inv_ref.at[spot], sems.at[j, at])
            )
            copies[j][-1].start()
    return copies


def turn_kernel(rows_ref, out_ref):
    _, _, _, z = place()
    for at in range(8):
        turned = (at % 2) * 4 + at // 2 % 2 * 2 + at // 4
        out_ref[at] = rows_ref[jnp.where((z & 1) == 1, turned, at)]


def turn(rows):
    out = jax.ShapeDtypeStruct(rows.shape, F32)
    return call(turn_kernel, out, (rows,), [VMEM], VMEM, [], LIM, 0.5)


def slice_kernel(rows_ref, inv_ref, out_ref, bhi, blo):
    for k in range(rows_ref.shape[0]):
        high, low = split(rows_ref[k])
        bhi[:, k * 128 : (k + 1) * 128] = high
        blo[:, k * 128 : (k + 1) * 128] = low
    for j in range(inv_ref.shape[0] // 256):
        cols, upto = slice(j * 256, (j + 1) * 256), slice(0, (j + 1) * 256)
        out_ref[:, cols] = dot3((bhi[:, upto], blo[:, upto]), split(inv_ref[cols, upto]))


def factor_slice(rows, inv_factor):
    count, tall, _ = rows.shape
    order = inv_factor.shape[0]
    return call(
        slice_kernel,
        jax.ShapeDtypeStruct((tall, order), F32),
        (rows, inv_factor),
        [VMEM, VMEM],
        VMEM,
        [pltpu.VMEM((tall, order), BF16), pltpu.VMEM((tall, order), BF16)],
        LIM,
        0.5,
    )


def factor_kernel(*rest):
    x, core, _, _ = place()
    order = [(0, 0), (0, 1)] + [(step, side) for side in (0, 1) for step in (1, 3, 2)]
    pieces, rest = rest[:-11], rest[-11:]
    inv_hbm, own_ref, halves, line_ref, f_ref, bhi, blo, inv_ref, lhi, llo, sems = rest
    local, step = line_ref.shape[1], 256
    copies = []
    for ref in pieces:
        for piece in range(ref.shape[0] // local):
            at = len(copies)
            rows = pl.ds(piece * local, local)
            copies.append(pltpu.make_async_copy(ref.at[rows, :], line_ref.at[at], sems.at[0, at // 2, at % 2]))
            copies[-1].start()
    ready = fetch_inverse(inv_hbm, inv_ref, sems.at[1], 2)
    for at, copy in enumerate(copies):
        copy.wait()
        step_x, side = order[at]
        lane = pl.multiple_of((((x + step_x) & 3) * 2 + (core ^ side)) * 128, 128)
        high, low = split(line_ref[at])
        bhi[:, pl.ds(lane, 128)] = high
        blo[:, pl.ds(lane, 128)] = low
    for m in range(local // step):
        rows = slice(m * step, (m + 1) * step)
        for j, arriving in enumerate(ready):
            cols, upto = slice(j * 256, (j + 1) * 256), slice(0, (j + 1) * 256)
            if m == 0:
                for copy in arriving:
                    copy.wait()
                high, low = split(inv_ref[cols, upto])
                lhi[cols, upto] = high
                llo[cols, upto] = low
            value = dot3((bhi[rows, upto], blo[rows, upto]), (lhi[cols, upto], llo[cols, upto]))
            high, low = split(value)
            halves[0, rows, cols] = high
            halves[1, rows, cols] = low
            for side in range(2):
                f_ref[2 * j + side, rows, :] = value[:, side * 128 : (side + 1) * 128]
    own_ref[...] = f_ref[x * 2 + core]


def factor(pieces, inv_factor):
    local, order = pieces[0].shape[0], inv_factor.shape[0]
    return call(
        factor_kernel,
        (
            jax.ShapeDtypeStruct((local, 128), F32),
            jax.ShapeDtypeStruct((2, local, order), BF16),
        ),
        (*pieces, inv_factor),
        [ANY] * (len(pieces) + 1),
        (VMEM, VMEM),
        [
            pltpu.VMEM((order // 128, local, 128), F32),
            pltpu.VMEM((order // 128, local, 128), F32),
            pltpu.VMEM((local, order), BF16),
            pltpu.VMEM((local, order), BF16),
            pltpu.VMEM((order, order), F32),
            pltpu.VMEM((order, order), BF16),
            pltpu.VMEM((order, order), BF16),
            pltpu.SemaphoreType.DMA((2, 4, 2)),
        ],
        LIM,
        GF_FACTOR,
    )


NEAR, FAR = (0, 1), (3, 2)


def sub_rows(sources):
    _, core, y, z = place()
    first, second = jnp.where(core == 0, z, y), jnp.where(core == 0, y, z)
    spot = []
    for move, steps in sources:
        p = (second + move) & 3
        for step in steps:
            q = (first + step) & 3
            other = (q >> 1) * 4 + (p >> 1) * 2 + (q & 1)
            spot.append(jnp.where(core == 0, (p >> 1) * 4 + q, other))
    group = pl.multiple_of(((second + sources[0][0]) & 1) * 8, 8)
    return group, spot


def split_pieces(pieces, chi, clo):
    for at, ref in enumerate(pieces):
        rows = slice(at * 256, (at + 1) * 256)
        high, low = split(ref[...])
        chi[rows, :] = high
        clo[rows, :] = low


def subtract(m, spot, f_ref, chi, clo, buf):
    step = 256
    lines = pl.ds(m * step, step)
    flat = buf.reshape(buf.shape[0] * 8, 128)
    for n in range(2):
        cols = slice(n * 256, (n + 1) * 256)
        product = dot3((f_ref[0, lines, :], f_ref[1, lines, :]), (chi[cols, :], clo[cols, :]))
        for j in range(2):
            spots = pl.ds(m * step * 8 + spot[2 * n + j], step, 8)
            flat[spots, :] = flat[spots, :] - product[:, j * 128 : (j + 1) * 128]


def open_kernel(sources, f_ref, near, far, a_ref, held, chi, clo, sems):
    group, spot = sub_rows(sources)
    copies = []
    for m in range(held.shape[0] // 256):
        lines = pl.ds(m * 256, 256)
        here = a_ref.at[lines, pl.ds(group, 8), :]
        copies.append(pltpu.make_async_copy(here, held.at[lines], sems.at[m]))
        copies[-1].start()
    split_pieces((near, far), chi, clo)
    for m, copy in enumerate(copies):
        copy.wait()
        subtract(m, spot, f_ref, chi, clo, held)


def close_kernel(sources, f_ref, near, far, held, *rest):
    out_ref, buf, chi, clo, sems = rest[-5:]
    group, spot = sub_rows(sources)
    split_pieces((near, far), chi, clo)
    copies = []
    for m in range(buf.shape[0] // 256):
        lines = pl.ds(m * 256, 256)
        buf[lines] = held[lines]
        subtract(m, spot, f_ref, chi, clo, buf)
        there = out_ref.at[lines, pl.ds(group, 8), :]
        copies.append(pltpu.make_async_copy(buf.at[lines], there, sems.at[m]))
        copies[-1].start()
    for copy in copies:
        copy.wait()


def update_scratch(local, order):
    return [
        pltpu.VMEM((512, order), BF16),
        pltpu.VMEM((512, order), BF16),
        pltpu.SemaphoreType.DMA((local // 256,)),
    ]


def open_group(sources, f, pieces, trailing):
    _, local, order = f.shape
    return call(
        functools.partial(open_kernel, sources),
        jax.ShapeDtypeStruct((local, 8, 128), F32),
        (f, *pieces, trailing),
        [VMEM, VMEM, VMEM, ANY],
        VMEM,
        update_scratch(local, order),
        LIM,
        GF_UPDATE,
    )


def close_group(sources, f, pieces, held, shape, so_far):
    _, local, order = f.shape
    after = () if so_far is None else (so_far,)
    return call(
        functools.partial(close_kernel, sources),
        jax.ShapeDtypeStruct(shape, F32),
        (f, *pieces, held, *after),
        [VMEM] * 4 + [ANY] * len(after),
        ANY,
        [pltpu.VMEM((local, 8, 128), F32), *update_scratch(local, order)],
        LIM,
        GF_UPDATE,
        {4: 0} if after else {},
    )


def pick_kernel(even_ref, odd_ref, out_ref):
    _, core, _, _ = place()

    @pl.when(core == 0)
    def _():
        out_ref[...] = even_ref[...]

    @pl.when(core == 1)
    def _():
        out_ref[...] = odd_ref[...]


def pick(even, odd):
    out = jax.ShapeDtypeStruct(even.shape, F32)
    return call(pick_kernel, out, (even, odd), [VMEM, VMEM], VMEM, [], LIM, 0.1)


def join_kernel(*refs):
    *parts, out_ref = refs
    rows = parts[0].shape[0]
    for at, part in enumerate(parts):
        out_ref[at * rows : (at + 1) * rows] = part[...]


def join(*parts):
    rows, cols = parts[0].shape
    return call(
        join_kernel,
        jax.ShapeDtypeStruct((len(parts) * rows, cols), F32),
        parts,
        [VMEM] * len(parts),
        VMEM,
        [],
        LIM,
        0.1,
    )


def per_device(trailing_block, panel_block, inv_factor):
    tiles, _, tile, cols_dev = panel_block.shape
    local = tiles * tile
    panel = panel_block.reshape(local, cols_dev)
    trailing = trailing_block.reshape(local, 16, 128)

    swapped = lax.ppermute(panel, BOTH, SWAP)
    line_ahead = lax.ppermute(panel, BOTH, x_axis(-1))
    line_behind = lax.ppermute(panel, BOTH, x_axis(1))
    mine = turn(panel.reshape(8, 128, cols_dev))
    halves = [list(range(8)), list(range(8, 16))]
    mine = lax.all_to_all(mine, "row", 0, 0, axis_index_groups=halves, tiled=True)
    mine, line_ahead, line_behind = lax.optimization_barrier((mine, line_ahead, line_behind))
    line_across = lax.ppermute(pick(line_ahead, line_behind), BOTH, OUTWARD)
    mine = lax.all_to_all(mine, "col", 0, 0, tiled=True)
    own = factor_slice(mine, inv_factor)

    ahead = lax.ppermute(own, BOTH, first_axis(-1))
    behind = lax.ppermute(own, BOTH, first_axis(1))
    across = lax.ppermute(own, BOTH, first_axis(2))

    line_ahead, line_behind, line_across, _ = lax.optimization_barrier(
        (line_ahead, line_behind, line_across, own)
    )
    others = join(line_ahead, line_behind, line_across)
    line = (panel, swapped, others, lax.ppermute(others, BOTH, SWAP))
    own_columns, f = factor(line, inv_factor)

    ahead, behind, across, f = lax.optimization_barrier((ahead, behind, across, f))
    near = join(own, ahead)
    near_ahead = lax.ppermute(near, BOTH, second_axis(-1))
    near_behind = lax.ppermute(near, BOTH, second_axis(1))
    far = join(behind, across)
    far_behind = lax.ppermute(far, BOTH, second_axis(1))
    far_ahead = lax.ppermute(far, BOTH, second_axis(-1))
    held = open_group(((0, NEAR), (0, FAR)), f, (near, far), trailing)
    near_ahead, far_behind, held = lax.optimization_barrier((near_ahead, far_behind, held))
    near_across = lax.ppermute(near_ahead, BOTH, second_axis(-1))
    far_across = lax.ppermute(far_behind, BOTH, second_axis(1))

    beside = open_group(((1, NEAR), (3, FAR)), f, (near_ahead, far_behind), trailing)
    pieces, shape = (far_ahead, near_behind), trailing.shape
    updated = close_group(((1, FAR), (3, NEAR)), f, pieces, beside, shape, None)
    pieces = (near_across, far_across)
    updated = close_group(((2, NEAR), (2, FAR)), f, pieces, held, shape, updated)
    return updated.reshape(trailing_block.shape), own_columns.reshape(panel_block.shape)


def solution(mesh):
    return jax.shard_map(
        per_device,
        mesh=mesh,
        in_specs=(P(None, "row", None, None, "col", None), P(None, "row", None, "col"), P()),
        out_specs=(P(None, "row", None, None, "col", None), P(None, "row", None, "col")),
        check_vma=False,
    )
```

```python
import functools

import jax
import jax.numpy as jnp
from jax import lax
from jax.experimental import pallas as pl
from jax.experimental.pallas import tpu as pltpu
from jax.sharding import PartitionSpec as P

BOTH = ("row", "col")
F32, BF16 = jnp.float32, jnp.bfloat16
LAST = (((1,), (1,)), ((), ()))
GF_FACTOR, GF_UPDATE = 4.0, 2.0
LIM = 40


def permutation(move):
    def index(x, y, z, core):
        return (y % 4 * 4 + z % 4) * 8 + x % 4 * 2 + core

    spots = [(x, y, z, core) for x in range(4) for y in range(4) for z in range(4) for core in (0, 1)]
    return [(index(*spot), index(*move(*spot))) for spot in spots]


def first_axis(step):
    return permutation(lambda x, y, z, core: (x, y + core * step, z + (1 - core) * step, core))


def second_axis(step):
    return permutation(lambda x, y, z, core: (x, y + (1 - core) * step, z + core * step, core))


def x_axis(step):
    return permutation(lambda x, y, z, core: (x + step, y, z, core))


OUTWARD = permutation(lambda x, y, z, core: (x - 1 + 2 * core, y, z, core))
SWAP = permutation(lambda x, y, z, core: (x, y, z, 1 - core))


def split(value):
    high = value.astype(BF16)
    return high, (value - high.astype(F32)).astype(BF16)


def dot3(left, right):
    dot = functools.partial(lax.dot_general, dimension_numbers=LAST, preferred_element_type=F32)
    return dot(left[0], right[0]) + (dot(left[0], right[1]) + dot(left[1], right[0]))


def call(kernel, out_shape, operands, in_specs, out_specs, scratch, megabytes, gigaflops, aliases=None):
    return pl.pallas_call(
        kernel,
        out_shape=out_shape,
        in_specs=in_specs,
        out_specs=out_specs,
        scratch_shapes=scratch,
        input_output_aliases=aliases or {},
        compiler_params=pltpu.CompilerParams(vmem_limit_bytes=megabytes * 2**20),
        cost_estimate=pl.CostEstimate(
            flops=int(gigaflops * 1e9), bytes_accessed=2**20, transcendentals=0
        ),
    )(*operands)


VMEM = pl.BlockSpec(memory_space=pltpu.VMEM)
ANY = pl.BlockSpec(memory_space=pl.ANY)


def place():
    row, col = lax.axis_index("row"), lax.axis_index("col")
    return col >> 1, col & 1, row >> 2, row & 3


def fetch_inverse(inv_hbm, inv_ref, sems, pieces):
    copies, wide = [], 256
    for j in range(inv_ref.shape[0] // wide):
        copies.append([])
        for at in range(pieces):
            tall = wide // pieces
            spot = (pl.ds(j * wide + at * tall, tall), pl.ds(0, (j + 1) * wide))
            copies[j].append(
                pltpu.make_async_copy(inv_hbm.at[spot], inv_ref.at[spot], sems.at[j, at])
            )
            copies[j][-1].start()
    return copies


def turn_kernel(rows_ref, out_ref):
    _, _, _, z = place()
    for at in range(8):
        turned = (at % 2) * 4 + at // 2 % 2 * 2 + at // 4
        out_ref[at] = rows_ref[jnp.where((z & 1) == 1, turned, at)]


def turn(rows):
    out = jax.ShapeDtypeStruct(rows.shape, F32)
    return call(turn_kernel, out, (rows,), [VMEM], VMEM, [], LIM, 0.5)


def slice_kernel(rows_ref, inv_ref, out_ref, bhi, blo):
    for k in range(rows_ref.shape[0]):
        high, low = split(rows_ref[k])
        bhi[:, k * 128 : (k + 1) * 128] = high
        blo[:, k * 128 : (k + 1) * 128] = low
    for j in range(inv_ref.shape[0] // 256):
        cols, upto = slice(j * 256, (j + 1) * 256), slice(0, (j + 1) * 256)
        out_ref[:, cols] = dot3((bhi[:, upto], blo[:, upto]), split(inv_ref[cols, upto]))


def factor_slice(rows, inv_factor):
    count, tall, _ = rows.shape
    order = inv_factor.shape[0]
    return call(
        slice_kernel,
        jax.ShapeDtypeStruct((tall, order), F32),
        (rows, inv_factor),
        [VMEM, VMEM],
        VMEM,
        [pltpu.VMEM((tall, order), BF16), pltpu.VMEM((tall, order), BF16)],
        LIM,
        0.5,
    )


def factor_kernel(*rest):
    x, core, _, _ = place()
    order = [(0, 0), (0, 1)] + [(step, side) for side in (0, 1) for step in (1, 3, 2)]
    pieces, rest = rest[:-11], rest[-11:]
    inv_hbm, own_ref, halves, line_ref, f_ref, bhi, blo, inv_ref, lhi, llo, sems = rest
    local, step = line_ref.shape[1], 256
    copies = []
    for ref in pieces:
        for piece in range(ref.shape[0] // local):
            at = len(copies)
            rows = pl.ds(piece * local, local)
            copies.append(pltpu.make_async_copy(ref.at[rows, :], line_ref.at[at], sems.at[0, at // 2, at % 2]))
            copies[-1].start()
    ready = fetch_inverse(inv_hbm, inv_ref, sems.at[1], 2)
    for at, copy in enumerate(copies):
        copy.wait()
        step_x, side = order[at]
        lane = pl.multiple_of((((x + step_x) & 3) * 2 + (core ^ side)) * 128, 128)
        high, low = split(line_ref[at])
        bhi[:, pl.ds(lane, 128)] = high
        blo[:, pl.ds(lane, 128)] = low
    for m in range(local // step):
        rows = slice(m * step, (m + 1) * step)
        for j, arriving in enumerate(ready):
            cols, upto = slice(j * 256, (j + 1) * 256), slice(0, (j + 1) * 256)
            if m == 0:
                for copy in arriving:
                    copy.wait()
                high, low = split(inv_ref[cols, upto])
                lhi[cols, upto] = high
                llo[cols, upto] = low
            value = dot3((bhi[rows, upto], blo[rows, upto]), (lhi[cols, upto], llo[cols, upto]))
            high, low = split(value)
            halves[0, rows, cols] = high
            halves[1, rows, cols] = low
            for side in range(2):
                f_ref[2 * j + side, rows, :] = value[:, side * 128 : (side + 1) * 128]
    own_ref[...] = f_ref[x * 2 + core]


def factor(pieces, inv_factor):
    local, order = pieces[0].shape[0], inv_factor.shape[0]
    return call(
        factor_kernel,
        (
            jax.ShapeDtypeStruct((local, 128), F32),
            jax.ShapeDtypeStruct((2, local, order), BF16),
        ),
        (*pieces, inv_factor),
        [ANY] * (len(pieces) + 1),
        (VMEM, VMEM),
        [
            pltpu.VMEM((order // 128, local, 128), F32),
            pltpu.VMEM((order // 128, local, 128), F32),
            pltpu.VMEM((local, order), BF16),
            pltpu.VMEM((local, order), BF16),
            pltpu.VMEM((order, order), F32),
            pltpu.VMEM((order, order), BF16),
            pltpu.VMEM((order, order), BF16),
            pltpu.SemaphoreType.DMA((2, 4, 2)),
        ],
        LIM,
        GF_FACTOR,
    )


def sub_rows(sources):
    _, core, y, z = place()
    first, second = jnp.where(core == 0, z, y), jnp.where(core == 0, y, z)
    spot = []
    for move, step in sources:
        p, q = (second + move) & 3, (first + step) & 3
        other = (q >> 1) * 4 + (p >> 1) * 2 + (q & 1)
        spot.append(jnp.where(core == 0, (p >> 1) * 4 + q, other))
    group = pl.multiple_of(((second + sources[0][0]) & 1) * 8, 8)
    return group, spot


def split_pieces(pieces, chi, clo):
    at = 0
    for ref in pieces:
        rows = slice(at, at + ref.shape[0])
        at += ref.shape[0]
        high, low = split(ref[...])
        chi[rows, :] = high
        clo[rows, :] = low


def subtract(m, spot, f_ref, chi, clo, buf):
    step = 256
    lines = pl.ds(m * step, step)
    flat = buf.reshape(buf.shape[0] * 8, 128)
    for n in range(len(spot) // 2):
        cols = slice(n * 256, (n + 1) * 256)
        product = dot3((f_ref[0, lines, :], f_ref[1, lines, :]), (chi[cols, :], clo[cols, :]))
        for j in range(2):
            spots = pl.ds(m * step * 8 + spot[2 * n + j], step, 8)
            flat[spots, :] = flat[spots, :] - product[:, j * 128 : (j + 1) * 128]


def open_kernel(sources, f_ref, *rest):
    *pieces, a_ref, buf, chi, clo, sems = rest
    group, spot = sub_rows(sources)
    copies = []
    for m in range(buf.shape[0] // 256):
        lines = pl.ds(m * 256, 256)
        here = a_ref.at[lines, pl.ds(group, 8), :]
        copies.append(pltpu.make_async_copy(here, buf.at[lines], sems.at[m]))
        copies[-1].start()
    split_pieces(pieces, chi, clo)
    for m, copy in enumerate(copies):
        copy.wait()
        subtract(m, spot, f_ref, chi, clo, buf)


def middle_kernel(sources, f_ref, *rest):
    *pieces, held, buf, chi, clo, sems = rest
    _, spot = sub_rows(sources)
    split_pieces(pieces, chi, clo)
    for m in range(buf.shape[0] // 256):
        lines = pl.ds(m * 256, 256)
        buf[lines] = held[lines]
        subtract(m, spot, f_ref, chi, clo, buf)


def close_kernel(sources, after, f_ref, *rest):
    *pieces, held = rest[: -5 - after]
    out_ref, buf, chi, clo, sems = rest[-5:]
    group, spot = sub_rows(sources)
    split_pieces(pieces, chi, clo)
    copies = []
    for m in range(buf.shape[0] // 256):
        lines = pl.ds(m * 256, 256)
        buf[lines] = held[lines]
        subtract(m, spot, f_ref, chi, clo, buf)
        there = out_ref.at[lines, pl.ds(group, 8), :]
        copies.append(pltpu.make_async_copy(buf.at[lines], there, sems.at[m]))
        copies[-1].start()
    for copy in copies:
        copy.wait()


def update_scratch(sources, f):
    _, local, order = f.shape
    return [
        pltpu.VMEM((128 * len(sources), order), BF16),
        pltpu.VMEM((128 * len(sources), order), BF16),
        pltpu.SemaphoreType.DMA((local // 256,)),
    ]


def open_group(sources, f, pieces, source):
    local = f.shape[1]
    fresh = source.shape[1] != 8
    return call(
        functools.partial(open_kernel if fresh else middle_kernel, sources),
        jax.ShapeDtypeStruct((local, 8, 128), F32),
        (f, *pieces, source),
        [VMEM] * (1 + len(pieces)) + [ANY if fresh else VMEM],
        VMEM,
        update_scratch(sources, f),
        LIM,
        GF_UPDATE * len(sources) / 4,
    )


def close_group(sources, f, pieces, held, shape, so_far):
    after = () if so_far is None else (so_far,)
    return call(
        functools.partial(close_kernel, sources, len(after)),
        jax.ShapeDtypeStruct(shape, F32),
        (f, *pieces, held, *after),
        [VMEM] * (2 + len(pieces)) + [ANY] * len(after),
        ANY,
        [pltpu.VMEM((f.shape[1], 8, 128), F32), *update_scratch(sources, f)],
        LIM,
        GF_UPDATE * len(sources) / 4,
        {2 + len(pieces): 0} if after else {},
    )


def halve_kernel(*refs):
    half = len(refs) // 3
    for at, ref in enumerate(refs[:half]):
        rows = ref.shape[0] // 2
        refs[half + 2 * at][...] = ref[:rows]
        refs[half + 2 * at + 1][...] = ref[rows:]


def halve(*blocks):
    rows, cols = blocks[0].shape
    count = 2 * len(blocks)
    part = jax.ShapeDtypeStruct((rows // 2, cols), F32)
    return call(halve_kernel, [part] * count, blocks, [VMEM] * len(blocks), [VMEM] * count, [], LIM, 0.1)


def pick_kernel(even_ref, odd_ref, out_ref):
    _, core, _, _ = place()

    @pl.when(core == 0)
    def _():
        out_ref[...] = even_ref[...]

    @pl.when(core == 1)
    def _():
        out_ref[...] = odd_ref[...]


def pick(even, odd):
    out = jax.ShapeDtypeStruct(even.shape, F32)
    return call(pick_kernel, out, (even, odd), [VMEM, VMEM], VMEM, [], LIM, 0.1)


def join_kernel(*refs):
    *parts, out_ref = refs
    rows = parts[0].shape[0]
    for at, part in enumerate(parts):
        out_ref[at * rows : (at + 1) * rows] = part[...]


def join(*parts):
    rows, cols = parts[0].shape
    return call(
        join_kernel,
        jax.ShapeDtypeStruct((len(parts) * rows, cols), F32),
        parts,
        [VMEM] * len(parts),
        VMEM,
        [],
        LIM,
        0.1,
    )


def per_device(trailing_block, panel_block, inv_factor):
    tiles, _, tile, cols_dev = panel_block.shape
    local = tiles * tile
    panel = panel_block.reshape(local, cols_dev)
    trailing = trailing_block.reshape(local, 16, 128)

    swapped = lax.ppermute(panel, BOTH, SWAP)
    line_ahead = lax.ppermute(panel, BOTH, x_axis(-1))
    line_behind = lax.ppermute(panel, BOTH, x_axis(1))
    mine = turn(panel.reshape(8, 128, cols_dev))
    halves = [list(range(8)), list(range(8, 16))]
    mine = lax.all_to_all(mine, "row", 0, 0, axis_index_groups=halves, tiled=True)
    mine, line_ahead, line_behind = lax.optimization_barrier((mine, line_ahead, line_behind))
    line_across = lax.ppermute(pick(line_ahead, line_behind), BOTH, OUTWARD)
    mine = lax.all_to_all(mine, "col", 0, 0, tiled=True)
    own = factor_slice(mine, inv_factor)

    ahead = lax.ppermute(own, BOTH, first_axis(-1))
    behind = lax.ppermute(own, BOTH, first_axis(1))
    across = lax.ppermute(own, BOTH, first_axis(2))

    line_ahead, line_behind, line_across, _ = lax.optimization_barrier(
        (line_ahead, line_behind, line_across, own)
    )
    others = join(line_ahead, line_behind, line_across)
    line = (panel, swapped, others, lax.ppermute(others, BOTH, SWAP))
    own_columns, f = factor(line, inv_factor)

    ahead, behind, across, f = lax.optimization_barrier((ahead, behind, across, f))
    near = join(own, ahead)
    near_ahead = lax.ppermute(near, BOTH, second_axis(-1))
    near_behind = lax.ppermute(near, BOTH, second_axis(1))
    far = join(behind, across)
    far_behind = lax.ppermute(far, BOTH, second_axis(1))
    far_ahead = lax.ppermute(far, BOTH, second_axis(-1))
    held = open_group(((0, 0), (0, 1), (0, 3), (0, 2)), f, (near, far), trailing)
    near_ahead, far_behind, held = lax.optimization_barrier((near_ahead, far_behind, held))
    relay = halve(near_ahead, far_behind)
    own_across = lax.ppermute(relay[0], BOTH, second_axis(-1))
    behind_across = lax.ppermute(relay[2], BOTH, second_axis(1))
    spots = ((1, 0), (1, 1), (3, 3), (3, 2))
    beside = open_group(spots, f, (near_ahead, far_behind), trailing)
    ahead, across, beside = lax.optimization_barrier((relay[1], relay[3], beside))
    ahead_across = lax.ppermute(ahead, BOTH, second_axis(-1))
    across_across = lax.ppermute(across, BOTH, second_axis(1))
    last = (own_across, behind_across, ahead_across, across_across)
    spots, shape = ((1, 3), (1, 2), (3, 0), (3, 1)), trailing.shape
    updated = close_group(spots, f, (far_ahead, near_behind), beside, shape, None)
    held = open_group(((2, 0), (2, 3)), f, last[:2], held)
    updated = close_group(((2, 1), (2, 2)), f, last[2:], held, shape, updated)
    return updated.reshape(trailing_block.shape), own_columns.reshape(panel_block.shape)


def solution(mesh):
    return jax.shard_map(
        per_device,
        mesh=mesh,
        in_specs=(P(None, "row", None, None, "col", None), P(None, "row", None, "col"), P()),
        out_specs=(P(None, "row", None, None, "col", None), P(None, "row", None, "col")),
        check_vma=False,
    )
```

```python
import functools

import jax
import jax.numpy as jnp
from jax import lax
from jax.experimental import pallas as pl
from jax.experimental.pallas import tpu as pltpu
from jax.sharding import PartitionSpec as P

BOTH = ("row", "col")
F32, BF16 = jnp.float32, jnp.bfloat16
LAST = (((1,), (1,)), ((), ()))
GF_FACTOR, GF_UPDATE = 4.0, 2.0
LIM = 38


def permutation(move):
    def index(x, y, z, core):
        return (y % 4 * 4 + z % 4) * 8 + x % 4 * 2 + core

    spots = [(x, y, z, core) for x in range(4) for y in range(4) for z in range(4) for core in (0, 1)]
    return [(index(*spot), index(*move(*spot))) for spot in spots]


def first_axis(step):
    return permutation(lambda x, y, z, core: (x, y + core * step, z + (1 - core) * step, core))


def second_axis(step):
    return permutation(lambda x, y, z, core: (x, y + (1 - core) * step, z + core * step, core))


def x_axis(step):
    return permutation(lambda x, y, z, core: (x + step, y, z, core))


OUTWARD = permutation(lambda x, y, z, core: (x - 1 + 2 * core, y, z, core))
SWAP = permutation(lambda x, y, z, core: (x, y, z, 1 - core))


def split(value):
    high = value.astype(BF16)
    return high, (value - high.astype(F32)).astype(BF16)


def dot3(left, right):
    dot = functools.partial(lax.dot_general, dimension_numbers=LAST, preferred_element_type=F32)
    return dot(left[0], right[0]) + (dot(left[0], right[1]) + dot(left[1], right[0]))


def call(kernel, out_shape, operands, in_specs, out_specs, scratch, megabytes, gigaflops, aliases=None):
    return pl.pallas_call(
        kernel,
        out_shape=out_shape,
        in_specs=in_specs,
        out_specs=out_specs,
        scratch_shapes=scratch,
        input_output_aliases=aliases or {},
        compiler_params=pltpu.CompilerParams(vmem_limit_bytes=megabytes * 2**20),
        cost_estimate=pl.CostEstimate(
            flops=int(gigaflops * 1e9), bytes_accessed=2**20, transcendentals=0
        ),
    )(*operands)


VMEM = pl.BlockSpec(memory_space=pltpu.VMEM)
ANY = pl.BlockSpec(memory_space=pl.ANY)


def place():
    row, col = lax.axis_index("row"), lax.axis_index("col")
    return col >> 1, col & 1, row >> 2, row & 3


def fetch_inverse(inv_hbm, inv_ref, sems, pieces):
    copies, wide = [], 256
    for j in range(inv_ref.shape[0] // wide):
        copies.append([])
        for at in range(pieces):
            tall = wide // pieces
            spot = (pl.ds(j * wide + at * tall, tall), pl.ds(0, (j + 1) * wide))
            copies[j].append(
                pltpu.make_async_copy(inv_hbm.at[spot], inv_ref.at[spot], sems.at[j, at])
            )
            copies[j][-1].start()
    return copies


def turn_kernel(rows_ref, out_ref):
    _, _, _, z = place()
    for at in range(8):
        turned = (at % 2) * 4 + at // 2 % 2 * 2 + at // 4
        out_ref[at] = rows_ref[jnp.where((z & 1) == 1, turned, at)]


def turn(rows):
    out = jax.ShapeDtypeStruct(rows.shape, F32)
    return call(turn_kernel, out, (rows,), [VMEM], VMEM, [], LIM, 0.5)


def slice_kernel(rows_ref, inv_ref, out_ref, bhi, blo):
    for k in range(rows_ref.shape[0]):
        high, low = split(rows_ref[k])
        bhi[:, k * 128 : (k + 1) * 128] = high
        blo[:, k * 128 : (k + 1) * 128] = low
    for j in range(inv_ref.shape[0] // 256):
        cols, upto = slice(j * 256, (j + 1) * 256), slice(0, (j + 1) * 256)
        out_ref[:, cols] = dot3((bhi[:, upto], blo[:, upto]), split(inv_ref[cols, upto]))


def factor_slice(rows, inv_factor):
    count, tall, _ = rows.shape
    order = inv_factor.shape[0]
    return call(
        slice_kernel,
        jax.ShapeDtypeStruct((tall, order), F32),
        (rows, inv_factor),
        [VMEM, VMEM],
        VMEM,
        [pltpu.VMEM((tall, order), BF16), pltpu.VMEM((tall, order), BF16)],
        LIM,
        0.5,
    )


def factor_kernel(*rest):
    x, core, _, _ = place()
    order = [(0, 0), (0, 1)] + [(step, side) for side in (0, 1) for step in (1, 3, 2)]
    pieces, rest = rest[:-11], rest[-11:]
    inv_hbm, own_ref, halves, line_ref, f_ref, bhi, blo, inv_ref, lhi, llo, sems = rest
    local, step = line_ref.shape[1], 256
    copies = []
    for ref in pieces:
        for piece in range(ref.shape[0] // local):
            at = len(copies)
            rows = pl.ds(piece * local, local)
            copies.append(pltpu.make_async_copy(ref.at[rows, :], line_ref.at[at], sems.at[0, at // 2, at % 2]))
            copies[-1].start()
    ready = fetch_inverse(inv_hbm, inv_ref, sems.at[1], 2)
    for at, copy in enumerate(copies):
        copy.wait()
        step_x, side = order[at]
        lane = pl.multiple_of((((x + step_x) & 3) * 2 + (core ^ side)) * 128, 128)
        high, low = split(line_ref[at])
        bhi[:, pl.ds(lane, 128)] = high
        blo[:, pl.ds(lane, 128)] = low
    for m in range(local // step):
        rows = slice(m * step, (m + 1) * step)
        for j, arriving in enumerate(ready):
            cols, upto = slice(j * 256, (j + 1) * 256), slice(0, (j + 1) * 256)
            if m == 0:
                for copy in arriving:
                    copy.wait()
                high, low = split(inv_ref[cols, upto])
                lhi[cols, upto] = high
                llo[cols, upto] = low
            value = dot3((bhi[rows, upto], blo[rows, upto]), (lhi[cols, upto], llo[cols, upto]))
            high, low = split(value)
            halves[0, rows, cols] = high
            halves[1, rows, cols] = low
            for side in range(2):
                f_ref[2 * j + side, rows, :] = value[:, side * 128 : (side + 1) * 128]
    own_ref[...] = f_ref[x * 2 + core]


def factor(pieces, inv_factor):
    local, order = pieces[0].shape[0], inv_factor.shape[0]
    return call(
        factor_kernel,
        (
            jax.ShapeDtypeStruct((local, 128), F32),
            jax.ShapeDtypeStruct((2, local, order), BF16),
        ),
        (*pieces, inv_factor),
        [ANY] * (len(pieces) + 1),
        (VMEM, VMEM),
        [
            pltpu.VMEM((order // 128, local, 128), F32),
            pltpu.VMEM((order // 128, local, 128), F32),
            pltpu.VMEM((local, order), BF16),
            pltpu.VMEM((local, order), BF16),
            pltpu.VMEM((order, order), F32),
            pltpu.VMEM((order, order), BF16),
            pltpu.VMEM((order, order), BF16),
            pltpu.SemaphoreType.DMA((2, 4, 2)),
        ],
        LIM,
        GF_FACTOR,
    )


def sub_rows(sources):
    _, core, y, z = place()
    first, second = jnp.where(core == 0, z, y), jnp.where(core == 0, y, z)
    spot = []
    for move, step in sources:
        p, q = (second + move) & 3, (first + step) & 3
        other = (q >> 1) * 4 + (p >> 1) * 2 + (q & 1)
        spot.append(jnp.where(core == 0, (p >> 1) * 4 + q, other))
    group = pl.multiple_of(((second + sources[0][0]) & 1) * 8, 8)
    return group, spot


def split_pieces(pieces, chi, clo):
    at = 0
    for ref in pieces:
        rows = slice(at, at + ref.shape[0])
        at += ref.shape[0]
        high, low = split(ref[...])
        chi[rows, :] = high
        clo[rows, :] = low


def subtract(m, spot, f_ref, chi, clo, buf):
    step = 256
    lines = pl.ds(m * step, step)
    flat = buf.reshape(buf.shape[0] * 8, 128)
    for n in range(len(spot) // 2):
        cols = slice(n * 256, (n + 1) * 256)
        product = dot3((f_ref[0, lines, :], f_ref[1, lines, :]), (chi[cols, :], clo[cols, :]))
        for j in range(2):
            spots = pl.ds(m * step * 8 + spot[2 * n + j], step, 8)
            flat[spots, :] = flat[spots, :] - product[:, j * 128 : (j + 1) * 128]


def open_kernel(sources, f_ref, *rest):
    *pieces, a_ref, buf, chi, clo, sems = rest
    group, spot = sub_rows(sources)
    copies = []
    for m in range(buf.shape[0] // 256):
        lines = pl.ds(m * 256, 256)
        here = a_ref.at[lines, pl.ds(group, 8), :]
        copies.append(pltpu.make_async_copy(here, buf.at[lines], sems.at[m]))
        copies[-1].start()
    split_pieces(pieces, chi, clo)
    for m, copy in enumerate(copies):
        copy.wait()
        subtract(m, spot, f_ref, chi, clo, buf)


def middle_kernel(sources, f_ref, *rest):
    *pieces, held, buf, chi, clo, sems = rest
    _, spot = sub_rows(sources)
    split_pieces(pieces, chi, clo)
    for m in range(buf.shape[0] // 256):
        lines = pl.ds(m * 256, 256)
        buf[lines] = held[lines]
        subtract(m, spot, f_ref, chi, clo, buf)


def close_kernel(sources, after, f_ref, *rest):
    *pieces, held = rest[: -5 - after]
    out_ref, buf, chi, clo, sems = rest[-5:]
    group, spot = sub_rows(sources)
    split_pieces(pieces, chi, clo)
    copies = []
    for m in range(buf.shape[0] // 256):
        lines = pl.ds(m * 256, 256)
        buf[lines] = held[lines]
        subtract(m, spot, f_ref, chi, clo, buf)
        there = out_ref.at[lines, pl.ds(group, 8), :]
        copies.append(pltpu.make_async_copy(buf.at[lines], there, sems.at[m]))
        copies[-1].start()
    for copy in copies:
        copy.wait()


def update_scratch(sources, f):
    _, local, order = f.shape
    return [
        pltpu.VMEM((128 * len(sources), order), BF16),
        pltpu.VMEM((128 * len(sources), order), BF16),
        pltpu.SemaphoreType.DMA((local // 256,)),
    ]


def open_group(sources, f, pieces, source):
    local = f.shape[1]
    fresh = source.shape[1] != 8
    return call(
        functools.partial(open_kernel if fresh else middle_kernel, sources),
        jax.ShapeDtypeStruct((local, 8, 128), F32),
        (f, *pieces, source),
        [VMEM] * (1 + len(pieces)) + [ANY if fresh else VMEM],
        VMEM,
        update_scratch(sources, f),
        LIM,
        GF_UPDATE * len(sources) / 4,
    )


def close_group(sources, f, pieces, held, shape, so_far):
    after = () if so_far is None else (so_far,)
    return call(
        functools.partial(close_kernel, sources, len(after)),
        jax.ShapeDtypeStruct(shape, F32),
        (f, *pieces, held, *after),
        [VMEM] * (2 + len(pieces)) + [ANY] * len(after),
        ANY,
        [pltpu.VMEM((f.shape[1], 8, 128), F32), *update_scratch(sources, f)],
        LIM,
        GF_UPDATE * len(sources) / 4,
        {2 + len(pieces): 0} if after else {},
    )


def halve_kernel(*refs):
    half = len(refs) // 3
    for at, ref in enumerate(refs[:half]):
        rows = ref.shape[0] // 2
        refs[half + 2 * at][...] = ref[:rows]
        refs[half + 2 * at + 1][...] = ref[rows:]


def halve(*blocks):
    rows, cols = blocks[0].shape
    count = 2 * len(blocks)
    part = jax.ShapeDtypeStruct((rows // 2, cols), F32)
    return call(halve_kernel, [part] * count, blocks, [VMEM] * len(blocks), [VMEM] * count, [], LIM, 0.1)


def pick_kernel(even_ref, odd_ref, out_ref):
    _, core, _, _ = place()

    @pl.when(core == 0)
    def _():
        out_ref[...] = even_ref[...]

    @pl.when(core == 1)
    def _():
        out_ref[...] = odd_ref[...]


def pick(even, odd):
    out = jax.ShapeDtypeStruct(even.shape, F32)
    return call(pick_kernel, out, (even, odd), [VMEM, VMEM], VMEM, [], LIM, 0.1)


def join_kernel(*refs):
    *parts, out_ref = refs
    rows = parts[0].shape[0]
    for at, part in enumerate(parts):
        out_ref[at * rows : (at + 1) * rows] = part[...]


def join(*parts):
    rows, cols = parts[0].shape
    return call(
        join_kernel,
        jax.ShapeDtypeStruct((len(parts) * rows, cols), F32),
        parts,
        [VMEM] * len(parts),
        VMEM,
        [],
        LIM,
        0.1,
    )


def per_device(trailing_block, panel_block, inv_factor):
    tiles, _, tile, cols_dev = panel_block.shape
    local = tiles * tile
    panel = panel_block.reshape(local, cols_dev)
    trailing = trailing_block.reshape(local, 16, 128)

    swapped = lax.ppermute(panel, BOTH, SWAP)
    line_ahead = lax.ppermute(panel, BOTH, x_axis(-1))
    line_behind = lax.ppermute(panel, BOTH, x_axis(1))
    mine = turn(panel.reshape(8, 128, cols_dev))
    halves = [list(range(8)), list(range(8, 16))]
    mine = lax.all_to_all(mine, "row", 0, 0, axis_index_groups=halves, tiled=True)
    mine, line_ahead, line_behind = lax.optimization_barrier((mine, line_ahead, line_behind))
    line_across = lax.ppermute(pick(line_ahead, line_behind), BOTH, OUTWARD)
    mine = lax.all_to_all(mine, "col", 0, 0, tiled=True)
    own = factor_slice(mine, inv_factor)

    ahead = lax.ppermute(own, BOTH, first_axis(-1))
    behind = lax.ppermute(own, BOTH, first_axis(1))
    across = lax.ppermute(own, BOTH, first_axis(2))

    line_ahead, line_behind, line_across, _ = lax.optimization_barrier(
        (line_ahead, line_behind, line_across, own)
    )
    others = join(line_ahead, line_behind, line_across)
    line = (panel, swapped, others, lax.ppermute(others, BOTH, SWAP))
    own_columns, f = factor(line, inv_factor)

    ahead, behind, across, f = lax.optimization_barrier((ahead, behind, across, f))
    near = join(own, ahead)
    near_ahead = lax.ppermute(near, BOTH, second_axis(-1))
    near_behind = lax.ppermute(near, BOTH, second_axis(1))
    far = join(behind, across)
    far_behind = lax.ppermute(far, BOTH, second_axis(1))
    far_ahead = lax.ppermute(far, BOTH, second_axis(-1))
    held = open_group(((0, 0), (0, 1), (0, 3), (0, 2)), f, (near, far), trailing)
    near_ahead, far_behind, held = lax.optimization_barrier((near_ahead, far_behind, held))
    relay = halve(near_ahead, far_behind)
    own_across = lax.ppermute(relay[0], BOTH, second_axis(-1))
    behind_across = lax.ppermute(relay[2], BOTH, second_axis(1))
    spots = ((1, 0), (1, 1), (3, 3), (3, 2))
    beside = open_group(spots, f, (near_ahead, far_behind), trailing)
    ahead, across, beside = lax.optimization_barrier((relay[1], relay[3], beside))
    ahead_across = lax.ppermute(ahead, BOTH, second_axis(-1))
    across_across = lax.ppermute(across, BOTH, second_axis(1))
    last = (own_across, behind_across, ahead_across, across_across)
    spots, shape = ((1, 3), (1, 2), (3, 0), (3, 1)), trailing.shape
    updated = close_group(spots, f, (far_ahead, near_behind), beside, shape, None)
    held = open_group(((2, 0), (2, 3)), f, last[:2], held)
    updated = close_group(((2, 1), (2, 2)), f, last[2:], held, shape, updated)
    return updated.reshape(trailing_block.shape), own_columns.reshape(panel_block.shape)


def solution(mesh):
    return jax.shard_map(
        per_device,
        mesh=mesh,
        in_specs=(P(None, "row", None, None, "col", None), P(None, "row", None, "col"), P()),
        out_specs=(P(None, "row", None, None, "col", None), P(None, "row", None, "col")),
        check_vma=False,
    )
```
